256 devices in a mesh: dp: 8 (over x, y_lo), tm: 32 (over y_hi, z, core).
Axes of the slice: x: 4, y: 4 (y_hi: 2, y_lo: 2; y = y_hi * 2 + y_lo), z: 8, core: 2. Of those that a mesh axis runs over, the one named last changes fastest.
Arguments:
- frames: bfloat16 [8, 16384, 1536], P('dp', 'tm'), may hold values from -30 to 30
- lengths: int32 [8], P('dp'), may hold values from 8192 to 16384
- ln_gain: float32 [1536], replicated, may hold values from 0.1 to 1.9
- w_query: bfloat16 [1536, 1536], P(None, ('dp', 'tm')), may hold values from -1 to 1
- w_key: bfloat16 [1536, 1536], P(None, ('dp', 'tm')), may hold values from -1 to 1
- w_value: bfloat16 [1536, 1536], P(None, ('dp', 'tm')), may hold values from -0.15625 to 0.15625
- w_out: bfloat16 [1536, 1536], P(None, ('dp', 'tm')), may hold values from -0.15625 to 0.15625
Outputs:
- result: bfloat16 [8, 16384, 1536], P('dp', 'tm')
The draws below stay inside these ranges and needn't reach their ends.
All inputs are finite; a program needn't handle non-finite values.
Results may differ from the reference program's by a relative error of at most 0.0033.
The reference program's roundings to bfloat16 on the way (of `normed`, `attn_probs` and `attended`) count: a program that leaves them out, or rounds other values in their place, can miss the bound.
Values may be sent and summed in bfloat16 or wider, within the bound.
A program may use at most 128 MiB of HBM per device.

```python
import math
import jax
import jax.numpy as jnp
from jax import lax

D = 1536
H = 16
HD = 96
W = 128
UTTS = 8
FRAMES = 16384


def projection_draw(key, salt):
    key = jax.random.fold_in(key, salt)
    own_part = jax.random.normal(key, (D, D), jnp.float32)
    mixed_draw = own_part / math.sqrt(D)
    return jnp.clip(mixed_draw, -1.0, 1.0).astype(jnp.bfloat16)


def draw_w_query(key, part):
    return projection_draw(key, 11)


def draw_w_key(key, part):
    return projection_draw(key, 12)


def draw_frames(key, part):
    key = jax.random.fold_in(key, 21)
    normal_part = jax.random.normal(key, (UTTS, FRAMES, D), jnp.float32)
    drawn = jnp.clip(normal_part, -6.0, 6.0)
    return drawn.astype(jnp.bfloat16)


def place_ends(values, stream_key, smallest, largest):
    longest = values.shape.index(max(values.shape))
    spots = []
    for shift in (0, 1):
        where = [jax.random.randint(jax.random.fold_in(stream_key, axis), (), 0, length) for axis, length in enumerate(values.shape)]
        where[longest] = (where[longest] + shift) % values.shape[longest]
        spots.append(tuple(where))
    return values.at[spots[0]].set(smallest).at[spots[1]].set(largest)


def shard_levels(own_key, extent, split, smallest, top_value):
    gain = 1.0
    for axis_at, blocks in split:
        steps = jax.random.uniform(jax.random.fold_in(jax.random.fold_in(own_key, 6), axis_at), (blocks,), jnp.float32, smallest / len(split), top_value / len(split))
        gain = gain * jnp.repeat(jnp.exp(steps), extent[axis_at] // blocks).reshape((-1,) + (1,) * (len(extent) - 1 - axis_at))
    return gain


def gaussian(stream_key, dims, scale, most, cuts=(), kind=jnp.bfloat16):
    result = scale * jax.random.normal(stream_key, dims, jnp.float32)
    if cuts:
        result = result * shard_levels(stream_key, dims, cuts, -0.22, 0.18)
    return jnp.clip(result, -most, most).astype(kind)


def setup_inputs(seed: int = 0) -> dict:
    splits = jax.random.split(jax.random.key(seed), 8)
    return {
        "frames": draw_frames(jax.random.fold_in(splits[7], 71), 0),
        "lengths": place_ends(jax.random.randint(splits[1], (UTTS,), FRAMES // 2, FRAMES + 1), jax.random.fold_in(splits[1], 1), FRAMES // 2, FRAMES).astype(jnp.int32),
        "ln_gain": jnp.clip(1.0 + 0.18 * jax.random.normal(splits[2], (D,), jnp.float32), 0.1, 1.9),
        "w_query": draw_w_query(jax.random.fold_in(splits[7], 71), 0),
        "w_key": draw_w_key(jax.random.fold_in(splits[7], 71), 0),
        "w_value": gaussian(splits[5], (D, D), D ** -0.5, 0.15625, ((1, 256),)),
        "w_out": gaussian(splits[6], (D, D), D ** -0.5, 0.15625, ((1, 256),)),
    }


EPSILON = 1e-05

def norm_rows(values, ln_gain):
    as_float = values.astype(jnp.float32)
    row_mean = lax.optimization_barrier(jnp.mean(as_float, axis=-1, keepdims=True))
    centered = as_float - row_mean
    row_var = lax.optimization_barrier(jnp.mean(centered * centered, axis=-1, keepdims=True))
    return (centered * lax.rsqrt(row_var + EPSILON) * ln_gain).astype(jnp.bfloat16)

def reference(frames, lengths, ln_gain, w_query, w_key, w_value, w_out):
    tile_rows = math.gcd(FRAMES, 512)
    num_tiles = FRAMES // tile_rows
    scale = 1.0 / math.sqrt(HD)

    def one_utterance(packed):
        utterance, length = packed
        normed = norm_rows(utterance, ln_gain)
        queries = jnp.dot(normed, w_query, preferred_element_type=jnp.float32).astype(jnp.bfloat16)
        key_rows = jnp.dot(normed, w_key, preferred_element_type=jnp.float32).astype(jnp.bfloat16)
        value_rows = jnp.dot(normed, w_value, preferred_element_type=jnp.float32).astype(jnp.bfloat16)
        padding = jnp.zeros((W, D), jnp.bfloat16)
        key_ext = jnp.concatenate([padding, key_rows, padding], axis=0)
        value_ext = jnp.concatenate([padding, value_rows, padding], axis=0)

        def attend_tile(tile_index):
            offset = (tile_index * tile_rows).astype(jnp.int32)
            query_tile = lax.dynamic_slice_in_dim(queries, offset, tile_rows, 0).reshape(tile_rows, H, HD)
            key_tile = lax.dynamic_slice_in_dim(key_ext, offset, tile_rows + 2 * W, 0).reshape(tile_rows + 2 * W, H, HD)
            value_tile = lax.dynamic_slice_in_dim(value_ext, offset, tile_rows + 2 * W, 0).reshape(tile_rows + 2 * W, H, HD)
            scores = jnp.einsum('qhd,khd->hqk', query_tile.astype(jnp.float32), key_tile.astype(jnp.float32)) * scale
            query_pos = offset + jnp.arange(tile_rows, dtype=jnp.int32)
            key_pos = offset - W + jnp.arange(tile_rows + 2 * W, dtype=jnp.int32)
            allowed = (jnp.abs(query_pos[:, None] - key_pos[None, :]) <= W) & (key_pos >= 0)[None, :] & (key_pos < length)[None, :]
            scores = scores + jnp.where(allowed, 0.0, -1000000000.0).astype(jnp.float32)[None]
            row_max = lax.optimization_barrier(jnp.max(scores, axis=-1, keepdims=True))
            shifted = jnp.exp(scores - row_max)
            attn_probs = (shifted / lax.optimization_barrier(jnp.sum(shifted, axis=-1, keepdims=True))).astype(jnp.bfloat16)
            attended = jnp.einsum('hqk,khd->qhd', attn_probs.astype(jnp.float32), value_tile.astype(jnp.float32))
            return attended.astype(jnp.bfloat16).reshape(tile_rows, D)
        attended = lax.map(attend_tile, jnp.arange(num_tiles, dtype=jnp.int32)).reshape(FRAMES, D)
        mixed_out = jnp.dot(attended, w_out, preferred_element_type=jnp.float32)
        summed = utterance.astype(jnp.float32) + mixed_out
        is_valid = jnp.arange(FRAMES, dtype=jnp.int32) < length
        return jnp.where(is_valid[:, None], summed, 0.0).astype(jnp.bfloat16)
    return lax.map(one_utterance, (frames, lengths))
```

```python
import math

import jax
import jax.numpy as jnp
from jax import lax
from jax.experimental import pallas as pl
from jax.experimental.pallas import tpu as pltpu
from jax.sharding import PartitionSpec as P

D = 1536
HALF = D // 2
H = 16
HD = 96
W = 128
ROWS = 512
EXT = ROWS + 2 * W
EPSILON = 1e-05
SCALE = 1.0 / math.sqrt(HD)
TQ = 256
TK = TQ + 2 * W
MESH = pl.DeviceIdType.MESH


def norm_rows(values, ln_gain):
    as_float = values.astype(jnp.float32)
    row_mean = jnp.mean(as_float, axis=-1, keepdims=True)
    centered = as_float - row_mean
    row_var = jnp.mean(centered * centered, axis=-1, keepdims=True)
    return (centered * lax.rsqrt(row_var + EPSILON) * ln_gain).astype(jnp.bfloat16)


def attend_head(q_t, k_t, v_t, bias_ref):
    pieces = []
    for t in range(ROWS // TQ):
        lo = t * TQ
        scores = lax.dot_general(
            k_t[:, lo : lo + TK],
            q_t[:, lo : lo + TQ],
            (((0,), (0,)), ((), ())),
            preferred_element_type=jnp.float32,
        )
        scores = scores * SCALE + bias_ref[t]
        shifted = jnp.exp(scores - jnp.max(scores, axis=0, keepdims=True))
        probs = (shifted * (1.0 / jnp.sum(shifted, axis=0, keepdims=True))).astype(jnp.bfloat16)
        pieces.append(
            jnp.dot(v_t[:, lo : lo + TK], probs, preferred_element_type=jnp.float32).astype(
                jnp.bfloat16
            )
        )
    return jnp.concatenate(pieces, axis=1)


def pick(index, options):
    value = options[0]
    for k, option in enumerate(options[1:], 1):
        value = jnp.where(index == k, option, value)
    return value


N_COPIES = 80


def body(len_ref, frames, gain_ref, pad_ref, out_ref, low, high, given, zbuf, w, obuf, wo, x_t, bias, att, send_sem, recv_sem):
    dp = lax.axis_index("dp")
    tm = lax.axis_index("tm")
    x, y = dp // 2, (tm // 16) * 2 + dp % 2
    z, core = (tm // 2) % 8, tm % 2

    def device(px, py, pz, pc):
        return (px * 2 + py % 2, (py // 2) * 16 + pz * 2 + pc)

    def moved(first, second):
        dx = jnp.where(core == 0, first, second)
        dy = jnp.where(core == 0, second, first)
        return (x + dx + 4) % 4, (y + dy + 4) % 4

    def plane_device(first, second):
        px, py = moved(first, second)
        return device(px, py, z, core)

    def plane_place(first, second):
        px, py = moved(first, second)
        return px * 4 + py

    partner = device(x, y, z, 1 - core)
    z_up, z_down = device(x, y, (z + 1) % 8, core), device(x, y, (z + 7) % 8, core)
    after, before = (dp, (tm + 1) % 32), (dp, (tm + 31) % 32)
    first_line = {k: plane_device(k, 0) for k in (-1, 1, 2)}
    second_line = {k: plane_device(0, k) for k in (-1, 1, 2)}
    peers = [*first_line.values(), *second_line.values(), z_up, z_down, partner, after, before]

    barrier = pltpu.get_barrier_semaphore()
    for peer in peers:
        pl.semaphore_signal(barrier, inc=1, device_id=peer, device_id_type=MESH)
    pl.semaphore_wait(barrier, len(peers))

    copies = {}

    def send(name, src, dst, peer):
        k = len(copies)
        copies[name] = pltpu.make_async_remote_copy(
            src_ref=src,
            dst_ref=dst,
            send_sem=send_sem.at[k],
            recv_sem=recv_sem.at[k],
            device_id=peer,
            device_id_type=MESH,
        )
        copies[name].start()

    def arrived(*names):
        for name in names:
            copies[name].wait_recv()

    send("swap", pad_ref.at[1 - core], given, partner)
    send("low", frames.at[pl.ds(ROWS - W, W)], low, after)
    send("high", frames.at[pl.ds(0, W)], high, before)

    first_pos = tm * ROWS
    length = len_ref[0]
    gain = gain_ref[...]

    def norm_block(ref, r, col):
        x_t[:, col : col + W] = norm_rows(ref[r : r + W], gain).T

    arrived("swap")
    mine, other = pad_ref[core], given[...]
    one = jnp.where(core == 0, mine, other)
    two = jnp.where(core == 0, other, mine)
    zbuf[z] = jnp.concatenate([one[:24], two[:24]], axis=0)
    own = plane_place(0, 0)
    obuf[core, z, own] = jnp.concatenate([one[24:], two[24:]], axis=0)

    send("zu1", zbuf.at[z], zbuf.at[z], z_up)
    send("zd1", zbuf.at[z], zbuf.at[z], z_down)
    for k in (-1, 1, 2):
        send(f"of{k}", obuf.at[core, z, own], obuf.at[core, z, own], first_line[k])

    norm_block(frames, 0, W)
    arrived("zu1", "zd1")
    for d in (2,):
        src = (z + 8 - (d - 1)) % 8
        send(f"zu{d}", zbuf.at[src], zbuf.at[src], z_up)
        src = (z + (d - 1)) % 8
        send(f"zd{d}", zbuf.at[src], zbuf.at[src], z_down)
    arrived("of-1", "of1", "of2")
    for i in (0, -1, 1, 2):
        place = plane_place(i, 0)
        for k in (-1, 1, 2):
            send(f"os{i},{k}", obuf.at[core, z, place], obuf.at[core, z, place], second_line[k])
    norm_block(frames, W, 2 * W)
    arrived("zu2", "zd2")
    src = (z + 6) % 8
    send("zu3", zbuf.at[src], zbuf.at[src], z_up)
    src = (z + 2) % 8
    send("zd3", zbuf.at[src], zbuf.at[src], z_down)
    norm_block(frames, 2 * W, 3 * W)
    arrived("zu3")
    src = (z + 5) % 8
    send("zu4", zbuf.at[src], zbuf.at[src], z_up)
    for i in (0, -1, 1, 2):
        arrived(*(f"os{i},{k}" for k in (-1, 1, 2)))
    send("ou1", obuf.at[core, z], obuf.at[core, z], z_up)
    send("od1", obuf.at[core, z], obuf.at[core, z], z_down)
    send("oc0", obuf.at[core, z], obuf.at[core, z], partner)
    norm_block(frames, 3 * W, 4 * W)
    arrived("zd3", "zu4")

    row = lax.broadcasted_iota(jnp.int32, (3 * HD, 8 * 48), 0)
    col = lax.broadcasted_iota(jnp.int32, (3 * HD, 8 * 48), 1)
    kind, unit, part = row // HD, (row % HD) // 6, row % 6
    source = (unit // 2) * 48 + (unit % 2) * 24 + kind * 8 + part
    order = jnp.where(col == source, 1.0, 0.0).astype(jnp.bfloat16)
    w[own, core] = jnp.dot(
        order, zbuf[...].reshape(8 * 48, HALF), preferred_element_type=jnp.float32
    ).astype(jnp.bfloat16)

    def slab(name, first, second, peer):
        ref = w.at[plane_place(first, second), core]
        send(name, ref, ref, peer)

    def lower(name, first, second, peer):
        ref = w.at[plane_place(first, second), core, pl.ds(0, 144)]
        send(name, ref, ref, peer)

    def upper(name, first, second, peer):
        ref = w.at[plane_place(first, second), core, pl.ds(144, 144)]
        send(name, ref, ref, peer)

    def share(first, second):
        slab(f"c{first},{second}", first, second, partner)

    share(0, 0)
    slab("f-", 0, 0, first_line[1])
    slab("f+", 0, 0, first_line[-1])
    slab("s0-", 0, 0, second_line[1])
    slab("s0+", 0, 0, second_line[-1])

    arrived("low", "high")
    norm_block(low, 0, 0)
    norm_block(high, 0, W + ROWS)
    for t in range(ROWS // TQ):
        key = lax.broadcasted_iota(jnp.int32, (TK, TQ), 0)
        query = lax.broadcasted_iota(jnp.int32, (TK, TQ), 1)
        key_pos = key + (first_pos + t * TQ - W)
        allowed = (
            (key - query >= 0) & (key - query <= 2 * W) & (key_pos >= 0) & (key_pos < length)
        )
        bias[t] = jnp.where(allowed, 0.0, -1e9).astype(jnp.float32)

    def heads(offsets):
        def one_head(k, carry):
            first = pick(k, [o[0] for o in offsets])
            second = pick(k, [o[1] for o in offsets])
            px, py = moved(first, second)
            place = px * 4 + py
            qkv = jnp.dot(w[place, 0], x_t[:HALF], preferred_element_type=jnp.float32)
            qkv += jnp.dot(w[place, 1], x_t[HALF:], preferred_element_type=jnp.float32)
            qkv = qkv.astype(jnp.bfloat16)
            att[px * 4 + (py % 2) * 2 + py // 2] = attend_head(
                qkv[:HD, W : W + ROWS], qkv[HD : 2 * HD], qkv[2 * HD :], bias
            )
            return carry

        lax.fori_loop(0, len(offsets), one_head, 0)

    def o_ring(d):
        arrived(f"ou{d}", f"od{d}")
        below, above = (z + 8 - d) % 8, (z + d) % 8
        if d < 3:
            send(f"ou{d + 1}", obuf.at[core, below], obuf.at[core, below], z_up)
            send(f"od{d + 1}", obuf.at[core, above], obuf.at[core, above], z_down)
        elif d == 3:
            ref = obuf.at[core, below, pl.ds(0, 8)]
            send("ou4", ref, ref, z_up)
            ref = obuf.at[core, above, pl.ds(8, 8)]
            send("od4", ref, ref, z_down)
        send(f"oc{d}", obuf.at[core, below], obuf.at[core, below], partner)
        if d < 4:
            send(f"oc-{d}", obuf.at[core, above], obuf.at[core, above], partner)

    arrived("c0,0")
    heads([(0, 0)])

    arrived("f-", "f+")
    lower("ff-", -1, 0, first_line[1])
    upper("ff+", 1, 0, first_line[-1])
    for i in (-1, 1):
        slab(f"s{i}-", i, 0, second_line[1])
        slab(f"s{i}+", i, 0, second_line[-1])
        share(i, 0)

    def second_step(i):
        arrived(f"s{i}-", f"s{i}+")
        lower(f"ss{i}-", i, -1, second_line[1])
        upper(f"ss{i}+", i, 1, second_line[-1])
        share(i, -1)
        share(i, 1)

    def second_end(i):
        arrived(f"ss{i}-", f"ss{i}+")
        share(i, 2)

    second_step(0)
    o_ring(1)
    arrived("c-1,0", "c1,0", "c0,-1", "c0,1")
    heads([(-1, 0), (1, 0)])
    arrived("ff-", "ff+")
    slab("s2-", 2, 0, second_line[1])
    slab("s2+", 2, 0, second_line[-1])
    share(2, 0)
    second_end(0)
    heads([(0, -1), (0, 1)])
    o_ring(2)
    arrived("c2,0", "c0,2")
    heads([(2, 0), (0, 2)])
    second_step(-1)
    second_step(1)
    o_ring(3)
    arrived("c-1,-1", "c-1,1", "c1,-1", "c1,1")
    heads([(-1, -1), (1, 1), (-1, 1), (1, -1)])
    second_step(2)
    second_end(-1)
    second_end(1)
    o_ring(4)
    arrived("c2,-1", "c2,1", "c-1,2", "c1,2")
    heads([(2, -1), (2, 1), (-1, 2), (1, 2)])
    second_end(2)

    arrived("oc0", "oc1", "oc2", "oc3", "oc4", "oc-1", "oc-2", "oc-3")
    row = lax.broadcasted_iota(jnp.int32, (HD, 8 * 16), 0)
    col = lax.broadcasted_iota(jnp.int32, (HD, 8 * 16), 1)
    unit, part = row // 6, row % 6
    order = jnp.where(col == unit * 8 + part, 1.0, 0.0).astype(jnp.bfloat16)
    for h in range(H):
        place = (h // 4) * 4 + (h % 2) * 2 + (h // 2) % 2
        for half in range(2):
            wo[h, :, half * HALF : (half + 1) * HALF] = jnp.dot(
                order,
                obuf[half, :, place].reshape(8 * 16, HALF),
                preferred_element_type=jnp.float32,
            ).astype(jnp.bfloat16)
    arrived("c2,2")
    heads([(2, 2)])

    att_rows = att[...].reshape(D, ROWS).T
    pos = first_pos + lax.broadcasted_iota(jnp.int32, (ROWS, 1), 0)
    for c in range(0, H, 4):
        mixed = lax.dot_general(
            att_rows,
            wo[c : c + 4].reshape(4 * HD, D),
            (((1,), (1,)), ((), ())),
            preferred_element_type=jnp.float32,
        )
        cols = slice(c * HD, (c + 4) * HD)
        summed = frames[:, cols].astype(jnp.float32) + mixed
        out_ref[:, cols] = jnp.where(pos < length, summed, 0.0).astype(jnp.bfloat16)

    for copy in copies.values():
        copy.wait_send()
    assert len(copies) <= N_COPIES


def per_device(frames, lengths, ln_gain, w_query, w_key, w_value, w_out):
    stack = jnp.stack([w.T for w in (w_query, w_key, w_value, w_out)])
    padded = jnp.pad(stack, ((0, 0), (0, 2), (0, 0))).reshape(32, 2, HALF).transpose(1, 0, 2)
    vmem = pl.BlockSpec(memory_space=pltpu.VMEM)
    bf16 = jnp.bfloat16
    result = pl.pallas_call(
        body,
        out_shape=jax.ShapeDtypeStruct((ROWS, D), bf16),
        in_specs=[pl.BlockSpec(memory_space=pltpu.SMEM), vmem, vmem, vmem],
        out_specs=vmem,
        scratch_shapes=[
            pltpu.VMEM((W, D), bf16),
            pltpu.VMEM((W, D), bf16),
            pltpu.VMEM((32, HALF), bf16),
            pltpu.VMEM((8, 48, HALF), bf16),
            pltpu.VMEM((H, 2, 3 * HD, HALF), bf16),
            pltpu.VMEM((2, 8, H, 16, HALF), bf16),
            pltpu.VMEM((H, HD, D), bf16),
            pltpu.VMEM((D, EXT), bf16),
            pltpu.VMEM((ROWS // TQ, TK, TQ), jnp.float32),
            pltpu.VMEM((H, HD, ROWS), bf16),
            pltpu.SemaphoreType.DMA((N_COPIES,)),
            pltpu.SemaphoreType.DMA((N_COPIES,)),
        ],
        compiler_params=pltpu.CompilerParams(
            collective_id=0, has_side_effects=True, vmem_limit_bytes=60 * 2**20
        ),
    )(lengths, frames[0], ln_gain[None], padded)
    return result[None]


def solution(mesh):
    in_specs = (
        P("dp", "tm", None),
        P("dp"),
        P(),
        P(None, ("dp", "tm")),
        P(None, ("dp", "tm")),
        P(None, ("dp", "tm")),
        P(None, ("dp", "tm")),
    )
    return jax.shard_map(
        per_device,
        mesh=mesh,
        in_specs=in_specs,
        out_specs=P("dp", "tm", None),
        check_vma=False,
    )
```

```python
import math

import jax
import jax.numpy as jnp
from jax import lax
from jax.experimental import pallas as pl
from jax.experimental.pallas import tpu as pltpu
from jax.sharding import PartitionSpec as P

D = 1536
HALF = D // 2
H = 16
HD = 96
W = 128
ROWS = 512
EXT = ROWS + 2 * W
EPSILON = 1e-05
SCALE = 1.0 / math.sqrt(HD)
TQ = 256
TK = TQ + 2 * W
MESH = pl.DeviceIdType.MESH


def norm_rows(values, ln_gain):
    as_float = values.astype(jnp.float32)
    row_mean = jnp.mean(as_float, axis=-1, keepdims=True)
    centered = as_float - row_mean
    row_var = jnp.mean(centered * centered, axis=-1, keepdims=True)
    return (centered * lax.rsqrt(row_var + EPSILON) * ln_gain).astype(jnp.bfloat16)


def attend_head(q_t, k_t, v_t, bias_ref):
    pieces = []
    blank = jnp.zeros((W, W), jnp.bfloat16)
    for t in range(ROWS // TQ):
        lo = t * TQ
        scores = lax.dot_general(
            k_t[:, lo : lo + TK],
            q_t[:, lo : lo + TQ],
            (((0,), (0,)), ((), ())),
            preferred_element_type=jnp.float32,
        )
        sides = []
        for n in range(2):
            part = scores[n * W : n * W + 3 * W, n * W : n * W + W]
            part = part * (SCALE * math.log2(math.e)) + bias_ref[2 * t + n]
            shifted = jnp.exp2(part - jnp.max(part, axis=0, keepdims=True))
            probs = shifted * (1.0 / jnp.sum(shifted, axis=0, keepdims=True))
            probs = probs.astype(jnp.bfloat16)
            sides.append(jnp.concatenate([blank, probs] if n else [probs, blank], axis=0))
        probs = jnp.concatenate(sides, axis=1)
        pieces.append(
            jnp.dot(v_t[:, lo : lo + TK], probs, preferred_element_type=jnp.float32).astype(
                jnp.bfloat16
            )
        )
    return jnp.concatenate(pieces, axis=1)


def pick(index, options):
    value = options[0]
    for k, option in enumerate(options[1:], 1):
        value = jnp.where(index == k, option, value)
    return value


N_COPIES = 128
LINE = (-1, 1, 2)
KEYS, REST = 0, 1
PART_ROWS = (HD, 2 * HD)


def body(len_ref, frames_hbm, gain_ref, wk_ref, wv_ref, wq_ref, wo_ref, out_hbm, frames, out, raw, pad, low, high, given, zk, zr, wk, wr, oline, obuf, wo, x_t, kbuf, bias, att, in_sem, out_sem, send_sem, recv_sem):
    dp = lax.axis_index("dp")
    tm = lax.axis_index("tm")
    x, y = dp // 2, (tm // 16) * 2 + dp % 2
    z, core = (tm // 2) % 8, tm % 2

    def device(px, py, pz, pc):
        return (px * 2 + py % 2, (py // 2) * 16 + pz * 2 + pc)

    def moved(first, second):
        dx = jnp.where(core == 0, first, second)
        dy = jnp.where(core == 0, second, first)
        return (x + dx + 4) % 4, (y + dy + 4) % 4

    def plane_device(first, second):
        px, py = moved(first, second)
        return device(px, py, z, core)

    def plane_place(first, second):
        px, py = moved(first, second)
        return px * 4 + py

    partner = device(x, y, 1 * z, 1 - core)
    z_line = {k: device(x, y, (z + k + 8) % 8, core) for k in (4, 3, -3, 2, -2, 1, -1)}
    after, before = (dp, (tm + 1) % 32), (dp, (tm + 31) % 32)
    first_line = {k: plane_device(k, 0) for k in LINE}
    second_line = {k: plane_device(0, k) for k in LINE}
    peers = [*first_line.values(), *second_line.values(), *z_line.values(), partner, after, before]

    fetch = pltpu.make_async_copy(frames_hbm, frames, in_sem)
    fetch.start()
    barrier = pltpu.get_barrier_semaphore()
    for peer in peers:
        pl.semaphore_signal(barrier, inc=1, device_id=peer, device_id_type=MESH)

    raw[...] = jnp.zeros_like(raw)
    for n, ref in enumerate((wk_ref, wv_ref, wq_ref, wo_ref)):
        raw[8 * n : 8 * n + 6] = ref[...].astype(jnp.float32)
    pad[0] = raw[:, :HALF].astype(jnp.bfloat16)
    pad[1] = raw[:, HALF:].astype(jnp.bfloat16)
    pl.semaphore_wait(barrier, len(peers))

    copies = {}

    def send(name, src, dst, peer):
        k = len(copies)
        copies[name] = pltpu.make_async_remote_copy(
            src_ref=src,
            dst_ref=dst,
            send_sem=send_sem.at[k],
            recv_sem=recv_sem.at[k],
            device_id=peer,
            device_id_type=MESH,
        )
        copies[name].start()

    def arrived(*names):
        for name in names:
            copies[name].wait_recv()

    send("swap", pad.at[1 - core], given, partner)

    first_pos = tm * ROWS
    length = len_ref[0]
    gain = gain_ref[...].reshape(1, D)

    def norm_block(ref, r, col):
        x_t[:, col : col + W] = norm_rows(ref[r : r + W], gain).T

    arrived("swap")
    mine, other = pad[core], given[...]
    one = jnp.where(core == 0, mine, other)
    two = jnp.where(core == 0, other, mine)
    own = plane_place(0, 0)
    zk[z] = jnp.concatenate([one[:8], two[:8]], axis=0)
    for k, peer in z_line.items():
        send(f"zk{k}", zk.at[z], zk.at[z], peer)
    along = jnp.where(core == 0, x, y)
    across = jnp.where(core == 0, y, x)
    oline[along] = jnp.concatenate([one[24:], two[24:]], axis=0)
    for k in LINE:
        send(f"of{k}", oline.at[along], oline.at[along], first_line[k])
    zr[z] = jnp.concatenate([one[8:24], two[8:24]], axis=0)
    fetch.wait()

    norm_block(frames, 0, W)
    norm_block(frames, W, 2 * W)

    def ordered(buf, kinds):
        rows, cols = kinds * HD, 8 * kinds * 16
        row = lax.broadcasted_iota(jnp.int32, (rows, cols), 0)
        col = lax.broadcasted_iota(jnp.int32, (rows, cols), 1)
        kind, unit, part = row // HD, (row % HD) // 6, row % 6
        source = (unit // 2) * (kinds * 16) + (unit % 2) * (kinds * 8) + kind * 8 + part
        order = jnp.where(col == source, 1.0, 0.0).astype(jnp.bfloat16)
        return jnp.dot(order, buf.reshape(cols, HALF), preferred_element_type=jnp.float32).astype(
            jnp.bfloat16
        )

    parts = (wk, wr)

    def slab(name, part, first, second, peer, lo=0, size=None):
        ref = parts[part].at[plane_place(first, second), core]
        if size is not None:
            ref = parts[part].at[plane_place(first, second), core, pl.ds(lo, size)]
        send(f"{name},{part}", ref, ref, peer)

    def share(part, first, second):
        slab(f"c{first},{second}", part, first, second, partner)

    def begin(part):
        slab("f-", part, 0, 0, first_line[1])
        slab("f+", part, 0, 0, first_line[-1])
        slab("s0-", part, 0, 0, second_line[1])
        slab("s0+", part, 0, 0, second_line[-1])
        share(part, 0, 0)

    def first_step(part):
        half = PART_ROWS[part] // 2
        arrived(f"f-,{part}", f"f+,{part}")
        slab("ff-", part, -1, 0, first_line[1], 0, half)
        slab("ff+", part, 1, 0, first_line[-1], half, half)
        share(part, -1, 0)
        share(part, 1, 0)

    def second_begin(part, i):
        slab(f"s{i}-", part, i, 0, second_line[1])
        slab(f"s{i}+", part, i, 0, second_line[-1])

    def first_end(part):
        arrived(f"ff-,{part}", f"ff+,{part}")
        share(part, 2, 0)

    def second_step(part, i):
        half = PART_ROWS[part] // 2
        arrived(f"s{i}-,{part}", f"s{i}+,{part}")
        slab(f"ss{i}-", part, i, -1, second_line[1], 0, half)
        slab(f"ss{i}+", part, i, 1, second_line[-1], half, half)
        share(part, i, -1)
        share(part, i, 1)

    def second_end(part, i):
        arrived(f"ss{i}-,{part}", f"ss{i}+,{part}")
        share(part, i, 2)

    def locate(k, offsets, n, together):
        first = pick(k, [o[0] for o in offsets[n::together]])
        second = pick(k, [o[1] for o in offsets[n::together]])
        px, py = moved(first, second)
        return px * 4 + py, px * 4 + (py % 2) * 2 + py // 2

    def project(ref, places):
        rows = jnp.concatenate(
            [jnp.concatenate([ref[place, 0], ref[place, 1]], axis=1) for place in places], axis=0
        )
        return jnp.dot(rows, x_t[...], preferred_element_type=jnp.float32).astype(jnp.bfloat16)

    def keys(*offsets):
        arrived(*(f"c{second},{first},{KEYS}" for first, second in offsets))

        def some_keys(k, carry):
            places, names = zip(*(locate(k, offsets, n, 2) for n in range(2)))
            k_t = project(wk, places)
            for n in range(2):
                kbuf[names[n]] = k_t[n * HD : (n + 1) * HD]
            return carry

        lax.fori_loop(0, len(offsets) // 2, some_keys, 0)

    def heads(*offsets):
        arrived(*(f"c{second},{first},{REST}" for first, second in offsets))
        together = 2 - len(offsets) % 2

        def some_heads(k, carry):
            places, names = zip(*(locate(k, offsets, n, together) for n in range(together)))
            vq = project(wr, places)
            for n in range(together):
                v_t, q_t = (vq[(2 * n + m) * HD : (2 * n + m + 1) * HD] for m in range(2))
                att[names[n]] = attend_head(q_t[:, W : W + ROWS], kbuf[names[n]], v_t, bias)
            return carry

        lax.fori_loop(0, len(offsets) // together, some_heads, 0)

    def o_send(name, place, half, peer):
        ref = obuf.at[core, place, pl.ds(2 * half, 2)]
        send(f"{name}{half}", ref, ref, peer)

    def o_share(k):
        ref = obuf.at[core, (z + k + 8) % 8]
        send(f"oc{k}", ref, ref, partner)

    def o_begin():
        arrived(*(f"os{k}" for k in LINE))
        for half in range(2):
            o_send("ou1.", z, half, z_line[1])
            o_send("od1.", z, half, z_line[-1])
        o_share(0)

    def o_ring(d, half):
        arrived(f"ou{d}.{half}", f"od{d}.{half}")
        below, above = (z + 8 - d) % 8, (z + d) % 8
        if d < 3 or half == 0:
            o_send(f"ou{d + 1}.", below, half, z_line[1])
        if d < 3 or half == 1:
            o_send(f"od{d + 1}.", above, half, z_line[-1])
        if half == 1:
            o_share(-d)
            o_share(d)

    def o_end():
        arrived("ou4.0", "od4.1")
        o_share(4)

    arrived(*(f"zk{k}" for k in z_line))
    for k, peer in z_line.items():
        send(f"zr{k}", zr.at[z], zr.at[z], peer)
    wk[own, core] = ordered(zk[...], 1)
    begin(KEYS)
    arrived(*(f"of{k}" for k in LINE))
    row = lax.broadcasted_iota(jnp.int32, (48, 64), 0)
    col = lax.broadcasted_iota(jnp.int32, (48, 64), 1)
    order = jnp.where(col == (row // 6) * 8 + row % 6, 1.0, 0.0).astype(jnp.bfloat16)
    obuf[core, z, across] = jnp.dot(
        order, oline[...].reshape(64, HALF), preferred_element_type=jnp.float32
    ).astype(jnp.bfloat16)
    for k in LINE:
        send(f"os{k}", obuf.at[core, z, across], obuf.at[core, z, across], second_line[k])
    norm_block(frames, 2 * W, 3 * W)
    first_step(KEYS)
    second_step(KEYS, 0)
    second_begin(KEYS, -1)
    second_begin(KEYS, 1)
    norm_block(frames, 3 * W, 4 * W)
    arrived(*(f"zr{k}" for k in z_line))
    wr[own, core] = ordered(zr[...], 2)
    begin(REST)
    send("low", frames_hbm.at[pl.ds(ROWS - W, W)], low, after)
    send("high", frames_hbm.at[pl.ds(0, W)], high, before)
    o_begin()
    first_end(KEYS)
    second_begin(KEYS, 2)
    second_end(KEYS, 0)
    for t in range(ROWS // W):
        key = lax.broadcasted_iota(jnp.int32, (3 * W, W), 0)
        query = lax.broadcasted_iota(jnp.int32, (3 * W, W), 1)
        key_pos = key + (first_pos + (t - 1) * W)
        allowed = (
            (key - query >= 0) & (key - query <= 2 * W) & (key_pos >= 0) & (key_pos < length)
        )
        bias[t] = jnp.where(allowed, 0.0, -1e9).astype(jnp.float32)
    arrived("low", "high")
    norm_block(low, 0, 0)
    norm_block(high, 0, W + ROWS)
    second_step(KEYS, -1)
    second_step(KEYS, 1)
    o_ring(1, 0)
    keys((0, 0), (-1, 0), (1, 0), (0, -1), (0, 1), (2, 0))
    o_ring(1, 1)
    first_step(REST)
    second_step(REST, 0)
    second_begin(REST, -1)
    second_begin(REST, 1)
    second_step(KEYS, 2)
    second_end(KEYS, -1)
    second_end(KEYS, 1)
    heads((0, 0))
    o_ring(2, 0)
    keys((0, 2), (-1, -1), (1, 1), (-1, 1))
    second_end(KEYS, 2)
    o_ring(2, 1)
    first_end(REST)
    second_begin(REST, 2)
    second_end(REST, 0)
    heads((-1, 0), (1, 0))
    o_ring(3, 0)
    heads((0, -1), (0, 1))
    second_step(REST, -1)
    o_ring(3, 1)
    keys((1, -1), (2, -1), (2, 1), (-1, 2), (1, 2), (2, 2))
    second_step(REST, 1)
    heads((2, 0), (0, 2))
    o_end()
    second_end(REST, -1)
    heads((-1, -1), (1, 1))
    second_step(REST, 2)
    second_end(REST, 1)
    heads((-1, 1), (1, -1))
    arrived(*(f"oc{k}" for k in range(-3, 5)))
    row = lax.broadcasted_iota(jnp.int32, (4 * HD, 8 * 48), 0)
    col = lax.broadcasted_iota(jnp.int32, (4 * HD, 8 * 48), 1)
    unit, part = (row % HD) // 12, row % 12
    order = jnp.where(col == unit * 48 + (row // HD) * 12 + part, 1.0, 0.0).astype(jnp.bfloat16)
    for half in range(2):
        for fixed in range(4):
            four = jnp.dot(
                order,
                obuf[half, :, fixed].reshape(8 * 48, HALF),
                preferred_element_type=jnp.float32,
            ).astype(jnp.bfloat16)
            for k in range(4):
                px, py = (fixed, k) if half else (k, fixed)
                head = px * 4 + (py % 2) * 2 + py // 2
                wo[head, :, half * HALF : (half + 1) * HALF] = four[k * HD : (k + 1) * HD]
    heads((2, -1), (-1, 2))
    second_end(REST, 2)
    heads((2, 1), (1, 2))
    heads((2, 2))

    att_rows = att[...].reshape(D, ROWS).T
    pos = first_pos + lax.broadcasted_iota(jnp.int32, (ROWS, 1), 0)
    stores = []
    for n, c in enumerate(range(0, H, 4)):
        mixed = lax.dot_general(
            att_rows,
            wo[c : c + 4].reshape(4 * HD, D),
            (((1,), (1,)), ((), ())),
            preferred_element_type=jnp.float32,
        )
        cols = pl.ds(c * HD, 4 * HD)
        summed = frames[:, cols].astype(jnp.float32) + mixed
        out[:, cols] = jnp.where(pos < length, summed, 0.0).astype(jnp.bfloat16)
        stores.append(pltpu.make_async_copy(out.at[:, cols], out_hbm.at[:, cols], out_sem.at[n]))
        stores[-1].start()

    for copy in copies.values():
        copy.wait_send()
    for store in stores:
        store.wait()


def per_device(frames, lengths, ln_gain, w_query, w_key, w_value, w_out):
    vmem = pl.BlockSpec(memory_space=pltpu.VMEM)
    anywhere = pl.BlockSpec(memory_space=pl.ANY)
    bf16 = jnp.bfloat16
    result = pl.pallas_call(
        body,
        out_shape=jax.ShapeDtypeStruct((ROWS, D), bf16),
        in_specs=[pl.BlockSpec(memory_space=pltpu.SMEM), anywhere, vmem, vmem, vmem, vmem, vmem],
        out_specs=anywhere,
        scratch_shapes=[
            pltpu.VMEM((ROWS, D), bf16),
            pltpu.VMEM((ROWS, D), bf16),
            pltpu.VMEM((32, D), jnp.float32),
            pltpu.VMEM((2, 32, HALF), bf16),
            pltpu.VMEM((W, D), bf16),
            pltpu.VMEM((W, D), bf16),
            pltpu.VMEM((32, HALF), bf16),
            pltpu.VMEM((8, 16, HALF), bf16),
            pltpu.VMEM((8, 32, HALF), bf16),
            pltpu.VMEM((H, 2, HD, HALF), bf16),
            pltpu.VMEM((H, 2, 2 * HD, HALF), bf16),
            pltpu.VMEM((4, 16, HALF), bf16),
            pltpu.VMEM((2, 8, 4, 48, HALF), bf16),
            pltpu.VMEM((H, HD, D), bf16),
            pltpu.VMEM((D, EXT), bf16),
            pltpu.VMEM((H, HD, EXT), bf16),
            pltpu.VMEM((ROWS // W, 3 * W, W), jnp.float32),
            pltpu.VMEM((H, HD, ROWS), bf16),
            pltpu.SemaphoreType.DMA,
            pltpu.SemaphoreType.DMA((4,)),
            pltpu.SemaphoreType.DMA((N_COPIES,)),
            pltpu.SemaphoreType.DMA((N_COPIES,)),
        ],
        compiler_params=pltpu.CompilerParams(
            collective_id=0, has_side_effects=True, vmem_limit_bytes=60 * 2**20
        ),
    )(lengths, frames[0], ln_gain, w_key.T, w_value.T, w_query.T, w_out.T)
    return result[None]


def solution(mesh):
    in_specs = (
        P("dp", "tm", None),
        P("dp"),
        P(),
        P(None, ("dp", "tm")),
        P(None, ("dp", "tm")),
        P(None, ("dp", "tm")),
        P(None, ("dp", "tm")),
    )
    return jax.shard_map(
        per_device,
        mesh=mesh,
        in_specs=in_specs,
        out_specs=P("dp", "tm", None),
        check_vma=False,
    )
```

```python
import math

import jax
import jax.numpy as jnp
from jax import lax
from jax.experimental import pallas as pl
from jax.experimental.pallas import tpu as pltpu
from jax.sharding import PartitionSpec as P

D = 1536
HALF = D // 2
H = 16
HD = 96
W = 128
ROWS = 512
EXT = ROWS + 2 * W
EPSILON = 1e-05
SCALE = 1.0 / math.sqrt(HD)
TQ = 256
TK = TQ + 2 * W
MESH = pl.DeviceIdType.MESH


def norm_rows(values, ln_gain):
    as_float = values.astype(jnp.float32)
    row_mean = jnp.mean(as_float, axis=-1, keepdims=True)
    centered = as_float - row_mean
    row_var = jnp.mean(centered * centered, axis=-1, keepdims=True)
    return (centered * lax.rsqrt(row_var + EPSILON) * ln_gain).astype(jnp.bfloat16)


def attend_head(q_t, k_t, v_t, bias_ref):
    pieces = []
    blank = jnp.zeros((W, W), jnp.bfloat16)
    for t in range(ROWS // TQ):
        lo = t * TQ
        scores = lax.dot_general(
            k_t[:, lo : lo + TK],
            q_t[:, lo : lo + TQ],
            (((0,), (0,)), ((), ())),
            preferred_element_type=jnp.float32,
        )
        sides = []
        for n in range(2):
            part = scores[n * W : n * W + 3 * W, n * W : n * W + W]
            part = part * (SCALE * math.log2(math.e)) + bias_ref[2 * t + n]
            shifted = jnp.exp2(part - jnp.max(part, axis=0, keepdims=True))
            probs = shifted * (1.0 / jnp.sum(shifted, axis=0, keepdims=True))
            probs = probs.astype(jnp.bfloat16)
            sides.append(jnp.concatenate([blank, probs] if n else [probs, blank], axis=0))
        probs = jnp.concatenate(sides, axis=1)
        pieces.append(
            jnp.dot(v_t[:, lo : lo + TK], probs, preferred_element_type=jnp.float32).astype(
                jnp.bfloat16
            )
        )
    return jnp.concatenate(pieces, axis=1)


def pick(index, options):
    value = options[0]
    for k, option in enumerate(options[1:], 1):
        value = jnp.where(index == k, option, value)
    return value


N_COPIES = 128
LINE = (-1, 1, 2)
KEYS, REST = 0, 1
PART_ROWS = (HD, 2 * HD)


def body(len_ref, frames_hbm, gain_ref, wk_ref, wv_ref, wq_ref, wo_ref, out_hbm, frames, out, raw, pad, low, high, given, zk, zr, wk, wr, oline, obuf, wo, x_t, kbuf, bias, att, in_sem, out_sem, send_sem, recv_sem):
    dp = lax.axis_index("dp")
    tm = lax.axis_index("tm")
    x, y = dp // 2, (tm // 16) * 2 + dp % 2
    z, core = (tm // 2) % 8, tm % 2

    def device(px, py, pz, pc):
        return (px * 2 + py % 2, (py // 2) * 16 + pz * 2 + pc)

    def moved(first, second):
        dx = jnp.where(core == 0, first, second)
        dy = jnp.where(core == 0, second, first)
        return (x + dx + 4) % 4, (y + dy + 4) % 4

    def plane_device(first, second):
        px, py = moved(first, second)
        return device(px, py, z, core)

    def plane_place(first, second):
        px, py = moved(first, second)
        return px * 4 + py

    partner = device(x, y, 1 * z, 1 - core)
    z_line = {k: device(x, y, (z + k + 8) % 8, core) for k in (4, 3, -3, 2, -2, 1, -1)}
    after, before = (dp, (tm + 1) % 32), (dp, (tm + 31) % 32)
    first_line = {k: plane_device(k, 0) for k in LINE}
    second_line = {k: plane_device(0, k) for k in LINE}
    peers = [*first_line.values(), *second_line.values(), *z_line.values(), partner, after, before]

    fetch = pltpu.make_async_copy(frames_hbm, frames, in_sem)
    fetch.start()
    barrier = pltpu.get_barrier_semaphore()
    for peer in peers:
        pl.semaphore_signal(barrier, inc=1, device_id=peer, device_id_type=MESH)

    raw[...] = jnp.zeros_like(raw)
    for n, ref in enumerate((wk_ref, wv_ref, wq_ref, wo_ref)):
        raw[8 * n : 8 * n + 6] = ref[...].astype(jnp.float32)
    pad[0] = raw[:, :HALF].astype(jnp.bfloat16)
    pad[1] = raw[:, HALF:].astype(jnp.bfloat16)
    pl.semaphore_wait(barrier, len(peers))

    copies = {}

    def send(name, src, dst, peer):
        k = len(copies)
        copies[name] = pltpu.make_async_remote_copy(
            src_ref=src,
            dst_ref=dst,
            send_sem=send_sem.at[k],
            recv_sem=recv_sem.at[k],
            device_id=peer,
            device_id_type=MESH,
        )
        copies[name].start()

    def arrived(*names):
        for name in names:
            copies[name].wait_recv()

    send("swap", pad.at[1 - core], given, partner)

    first_pos = tm * ROWS
    length = len_ref[0]
    gain = gain_ref[...].reshape(1, D)

    def norm_block(ref, r, col):
        x_t[:, col : col + W] = norm_rows(ref[r : r + W], gain).T

    arrived("swap")
    mine, other = pad[core], given[...]
    one = jnp.where(core == 0, mine, other)
    two = jnp.where(core == 0, other, mine)
    own = plane_place(0, 0)
    zk[z] = jnp.concatenate([one[:8], two[:8]], axis=0)
    for k, peer in z_line.items():
        send(f"zk{k}", zk.at[z], zk.at[z], peer)
    along = jnp.where(core == 0, x, y)
    across = jnp.where(core == 0, y, x)
    oline[along] = jnp.concatenate([one[24:], two[24:]], axis=0)
    for k in LINE:
        send(f"of{k}", oline.at[along], oline.at[along], first_line[k])
    row = lax.broadcasted_iota(jnp.int32, (24, 32), 0)
    col = lax.broadcasted_iota(jnp.int32, (24, 32), 1)
    order = jnp.where(col == (row // 6) * 8 + row % 6, 1.0, 0.0).astype(jnp.bfloat16)
    packed = jnp.dot(
        order,
        jnp.concatenate([one[8:24], two[8:24]], axis=0),
        preferred_element_type=jnp.float32,
    )
    zr[z, :, :HALF] = packed[:16].astype(jnp.bfloat16)
    zr[z, :, HALF:] = jnp.concatenate(
        [packed[16:, : HALF // 2], packed[16:, HALF // 2 :]], axis=0
    ).astype(jnp.bfloat16)
    fetch.wait()

    norm_block(frames, 0, W)
    norm_block(frames, W, 2 * W)

    def chosen(rows, source, buf):
        col = lax.broadcasted_iota(jnp.int32, (rows, buf.shape[0]), 1)
        order = jnp.where(col == source, 1.0, 0.0).astype(jnp.bfloat16)
        return jnp.dot(order, buf, preferred_element_type=jnp.float32)

    def ordered_keys():
        row = lax.broadcasted_iota(jnp.int32, (HD, 8 * 16), 0)
        source = (row // 12) * 16 + (row % 12 // 6) * 8 + row % 6
        return chosen(HD, source, zk[...].reshape(8 * 16, HALF)).astype(jnp.bfloat16)

    def ordered_rest():
        row = lax.broadcasted_iota(jnp.int32, (2 * HD, 8 * 16), 0)
        kind, chip, part = row // HD, (row % HD) // 12, row % 12
        local = (part // 6) * 12 + kind * 6 + part % 6
        base = chip * 16
        wide = zr[:, :, :HALF].reshape(8 * 16, HALF)
        tail = zr[:, :, HALF:].reshape(8 * 16, HALF // 2)
        first = chosen(2 * HD, jnp.where(local < 16, base + local, -1), wide)
        left = chosen(2 * HD, jnp.where(local < 16, -1, base + local - 16), tail)
        right = chosen(2 * HD, jnp.where(local < 16, -1, base + local - 8), tail)
        return (first + jnp.concatenate([left, right], axis=1)).astype(jnp.bfloat16)

    parts = (wk, wr)

    def slab(name, part, first, second, peer, lo=0, size=None):
        ref = parts[part].at[plane_place(first, second), core]
        if size is not None:
            ref = parts[part].at[plane_place(first, second), core, pl.ds(lo, size)]
        send(f"{name},{part}", ref, ref, peer)

    def share(part, first, second):
        slab(f"c{first},{second}", part, first, second, partner)

    def begin(part):
        slab("f-", part, 0, 0, first_line[1])
        slab("f+", part, 0, 0, first_line[-1])
        slab("s0-", part, 0, 0, second_line[1])
        slab("s0+", part, 0, 0, second_line[-1])
        share(part, 0, 0)

    def first_step(part):
        half = PART_ROWS[part] // 2
        arrived(f"f-,{part}", f"f+,{part}")
        slab("ff-", part, -1, 0, first_line[1], 0, half)
        slab("ff+", part, 1, 0, first_line[-1], half, half)
        share(part, -1, 0)
        share(part, 1, 0)

    def second_begin(part, i):
        slab(f"s{i}-", part, i, 0, second_line[1])
        slab(f"s{i}+", part, i, 0, second_line[-1])

    def first_end(part):
        arrived(f"ff-,{part}", f"ff+,{part}")
        share(part, 2, 0)

    def second_step(part, i):
        half = PART_ROWS[part] // 2
        arrived(f"s{i}-,{part}", f"s{i}+,{part}")
        slab(f"ss{i}-", part, i, -1, second_line[1], 0, half)
        slab(f"ss{i}+", part, i, 1, second_line[-1], half, half)
        share(part, i, -1)
        share(part, i, 1)

    def second_end(part, i):
        arrived(f"ss{i}-,{part}", f"ss{i}+,{part}")
        share(part, i, 2)

    def locate(k, offsets, n, together):
        first = pick(k, [o[0] for o in offsets[n::together]])
        second = pick(k, [o[1] for o in offsets[n::together]])
        px, py = moved(first, second)
        return px * 4 + py, px * 4 + (py % 2) * 2 + py // 2

    def project(ref, places):
        rows = jnp.concatenate(
            [jnp.concatenate([ref[place, 0], ref[place, 1]], axis=1) for place in places], axis=0
        )
        return jnp.dot(rows, x_t[...], preferred_element_type=jnp.float32).astype(jnp.bfloat16)

    def keys(*offsets):
        arrived(*(f"c{second},{first},{KEYS}" for first, second in offsets))

        def some_keys(k, carry):
            places, names = zip(*(locate(k, offsets, n, 2) for n in range(2)))
            k_t = project(wk, places)
            for n in range(2):
                kbuf[names[n]] = k_t[n * HD : (n + 1) * HD]
            return carry

        lax.fori_loop(0, len(offsets) // 2, some_keys, 0)

    def heads(*offsets):
        arrived(*(f"c{second},{first},{REST}" for first, second in offsets))
        together = 2 - len(offsets) % 2

        def some_heads(k, carry):
            places, names = zip(*(locate(k, offsets, n, together) for n in range(together)))
            vq = project(wr, places)
            for n in range(together):
                v_t, q_t = (vq[(2 * n + m) * HD : (2 * n + m + 1) * HD] for m in range(2))
                att[names[n]] = attend_head(q_t[:, W : W + ROWS], kbuf[names[n]], v_t, bias)
            return carry

        lax.fori_loop(0, len(offsets) // together, some_heads, 0)

    def o_send(name, place, half, peer):
        ref = obuf.at[core, place, pl.ds(2 * half, 2)]
        send(f"{name}{half}", ref, ref, peer)

    def o_share(k):
        ref = obuf.at[core, (z + k + 8) % 8]
        send(f"oc{k}", ref, ref, partner)

    def o_begin():
        arrived(*(f"os{k}" for k in LINE))
        for half in range(2):
            o_send("ou1.", z, half, z_line[1])
            o_send("od1.", z, half, z_line[-1])
        o_share(0)

    def o_ring(d, half):
        arrived(f"ou{d}.{half}", f"od{d}.{half}")
        below, above = (z + 8 - d) % 8, (z + d) % 8
        if d < 3 or half == 0:
            o_send(f"ou{d + 1}.", below, half, z_line[1])
        if d < 3 or half == 1:
            o_send(f"od{d + 1}.", above, half, z_line[-1])
        if half == 1:
            o_share(-d)
            o_share(d)

    def o_end():
        arrived("ou4.0", "od4.1")
        o_share(4)

    arrived(*(f"zk{k}" for k in z_line))
    for k, peer in z_line.items():
        send(f"zr{k}", zr.at[z], zr.at[z], peer)
    wk[own, core] = ordered_keys()
    begin(KEYS)
    arrived(*(f"of{k}" for k in LINE))
    row = lax.broadcasted_iota(jnp.int32, (48, 64), 0)
    col = lax.broadcasted_iota(jnp.int32, (48, 64), 1)
    order = jnp.where(col == (row // 6) * 8 + row % 6, 1.0, 0.0).astype(jnp.bfloat16)
    obuf[core, z, across] = jnp.dot(
        order, oline[...].reshape(64, HALF), preferred_element_type=jnp.float32
    ).astype(jnp.bfloat16)
    for k in LINE:
        send(f"os{k}", obuf.at[core, z, across], obuf.at[core, z, across], second_line[k])
    norm_block(frames, 2 * W, 3 * W)
    first_step(KEYS)
    second_step(KEYS, 0)
    second_begin(KEYS, -1)
    second_begin(KEYS, 1)
    norm_block(frames, 3 * W, 4 * W)
    for t in range(ROWS // W):
        key = lax.broadcasted_iota(jnp.int32, (3 * W, W), 0)
        query = lax.broadcasted_iota(jnp.int32, (3 * W, W), 1)
        key_pos = key + (first_pos + (t - 1) * W)
        allowed = (
            (key - query >= 0) & (key - query <= 2 * W) & (key_pos >= 0) & (key_pos < length)
        )
        bias[t] = jnp.where(allowed, 0.0, -1e9).astype(jnp.float32)
    arrived(*(f"zr{k}" for k in z_line))
    wr[own, core] = ordered_rest()
    begin(REST)
    send("low", frames_hbm.at[pl.ds(ROWS - W, W)], low, after)
    send("high", frames_hbm.at[pl.ds(0, W)], high, before)
    o_begin()
    first_end(KEYS)
    second_begin(KEYS, 2)
    second_end(KEYS, 0)
    second_step(KEYS, -1)
    second_step(KEYS, 1)
    arrived("low", "high")
    norm_block(low, 0, 0)
    norm_block(high, 0, W + ROWS)
    second_step(KEYS, 2)
    second_end(KEYS, -1)
    second_end(KEYS, 1)
    keys((0, 0), (-1, 0), (1, 0), (0, -1), (0, 1), (2, 0))
    first_step(REST)
    second_step(REST, 0)
    second_begin(REST, -1)
    second_begin(REST, 1)
    o_ring(1, 0)
    heads((0, 0))
    second_end(KEYS, 2)
    o_ring(1, 1)
    keys((0, 2), (-1, -1), (1, 1), (-1, 1))
    first_end(REST)
    second_begin(REST, 2)
    second_end(REST, 0)
    o_ring(2, 0)
    heads((-1, 0), (1, 0))
    o_ring(2, 1)
    second_step(REST, -1)
    heads((0, -1), (0, 1))
    second_step(REST, 1)
    o_ring(3, 0)
    heads((2, 0), (0, 2))
    o_ring(3, 1)
    second_end(REST, -1)
    keys((1, -1), (2, -1), (2, 1), (-1, 2), (1, 2), (2, 2))
    second_step(REST, 2)
    heads((-1, -1), (1, 1))
    second_end(REST, 1)
    o_end()
    heads((-1, 1), (1, -1))
    arrived(*(f"oc{k}" for k in range(-3, 5)))
    row = lax.broadcasted_iota(jnp.int32, (4 * HD, 8 * 48), 0)
    col = lax.broadcasted_iota(jnp.int32, (4 * HD, 8 * 48), 1)
    unit, part = (row % HD) // 12, row % 12
    order = jnp.where(col == unit * 48 + (row // HD) * 12 + part, 1.0, 0.0).astype(jnp.bfloat16)
    for half in range(2):
        for fixed in range(4):
            four = jnp.dot(
                order,
                obuf[half, :, fixed].reshape(8 * 48, HALF),
                preferred_element_type=jnp.float32,
            ).astype(jnp.bfloat16)
            for k in range(4):
                px, py = (fixed, k) if half else (k, fixed)
                head = px * 4 + (py % 2) * 2 + py // 2
                wo[head, :, half * HALF : (half + 1) * HALF] = four[k * HD : (k + 1) * HD]
    heads((2, -1), (-1, 2))
    second_end(REST, 2)
    heads((2, 1), (1, 2))
    heads((2, 2))

    att_rows = att[...].reshape(D, ROWS).T
    pos = first_pos + lax.broadcasted_iota(jnp.int32, (ROWS, 1), 0)
    stores = []
    for n, c in enumerate(range(0, H, 4)):
        mixed = lax.dot_general(
            att_rows,
            wo[c : c + 4].reshape(4 * HD, D),
            (((1,), (1,)), ((), ())),
            preferred_element_type=jnp.float32,
        )
        cols = pl.ds(c * HD, 4 * HD)
        summed = frames[:, cols].astype(jnp.float32) + mixed
        out[:, cols] = jnp.where(pos < length, summed, 0.0).astype(jnp.bfloat16)
        stores.append(pltpu.make_async_copy(out.at[:, cols], out_hbm.at[:, cols], out_sem.at[n]))
        stores[-1].start()

    for copy in copies.values():
        copy.wait_send()
    for store in stores:
        store.wait()


def per_device(frames, lengths, ln_gain, w_query, w_key, w_value, w_out):
    vmem = pl.BlockSpec(memory_space=pltpu.VMEM)
    anywhere = pl.BlockSpec(memory_space=pl.ANY)
    bf16 = jnp.bfloat16
    result = pl.pallas_call(
        body,
        out_shape=jax.ShapeDtypeStruct((ROWS, D), bf16),
        in_specs=[pl.BlockSpec(memory_space=pltpu.SMEM), anywhere, vmem, vmem, vmem, vmem, vmem],
        out_specs=anywhere,
        scratch_shapes=[
            pltpu.VMEM((ROWS, D), bf16),
            pltpu.VMEM((ROWS, D), bf16),
            pltpu.VMEM((32, D), jnp.float32),
            pltpu.VMEM((2, 32, HALF), bf16),
            pltpu.VMEM((W, D), bf16),
            pltpu.VMEM((W, D), bf16),
            pltpu.VMEM((32, HALF), bf16),
            pltpu.VMEM((8, 16, HALF), bf16),
            pltpu.VMEM((8, 16, 3 * HALF // 2), bf16),
            pltpu.VMEM((H, 2, HD, HALF), bf16),
            pltpu.VMEM((H, 2, 2 * HD, HALF), bf16),
            pltpu.VMEM((4, 16, HALF), bf16),
            pltpu.VMEM((2, 8, 4, 48, HALF), bf16),
            pltpu.VMEM((H, HD, D), bf16),
            pltpu.VMEM((D, EXT), bf16),
            pltpu.VMEM((H, HD, EXT), bf16),
            pltpu.VMEM((ROWS // W, 3 * W, W), jnp.float32),
            pltpu.VMEM((H, HD, ROWS), bf16),
            pltpu.SemaphoreType.DMA,
            pltpu.SemaphoreType.DMA((4,)),
            pltpu.SemaphoreType.DMA((N_COPIES,)),
            pltpu.SemaphoreType.DMA((N_COPIES,)),
        ],
        compiler_params=pltpu.CompilerParams(
            collective_id=0, has_side_effects=True, vmem_limit_bytes=60 * 2**20
        ),
    )(lengths, frames[0], ln_gain, w_key.T, w_value.T, w_query.T, w_out.T)
    return result[None]


def solution(mesh):
    in_specs = (
        P("dp", "tm", None),
        P("dp"),
        P(),
        P(None, ("dp", "tm")),
        P(None, ("dp", "tm")),
        P(None, ("dp", "tm")),
        P(None, ("dp", "tm")),
    )
    return jax.shard_map(
        per_device,
        mesh=mesh,
        in_specs=in_specs,
        out_specs=P("dp", "tm", None),
        check_vma=False,
    )
```

```python
import math

import jax
import jax.numpy as jnp
from jax import lax
from jax.experimental import pallas as pl
from jax.experimental.pallas import tpu as pltpu
from jax.sharding import PartitionSpec as P

D = 1536
HALF = D // 2
H = 16
HD = 96
W = 128
ROWS = 512
EXT = ROWS + 2 * W
EPSILON = 1e-05
SCALE = 1.0 / math.sqrt(HD)
TQ = 256
TK = TQ + 2 * W
MESH = pl.DeviceIdType.MESH


def norm_rows(values, ln_gain):
    as_float = values.astype(jnp.float32)
    row_mean = jnp.mean(as_float, axis=-1, keepdims=True)
    centered = as_float - row_mean
    row_var = jnp.mean(centered * centered, axis=-1, keepdims=True)
    return (centered * lax.rsqrt(row_var + EPSILON) * ln_gain).astype(jnp.bfloat16)


def attend_head(q_t, k_t, v_t, bias_ref):
    pieces = []
    blank = jnp.zeros((W, W), jnp.bfloat16)
    for t in range(ROWS // TQ):
        lo = t * TQ
        scores = lax.dot_general(
            k_t[:, lo : lo + TK],
            q_t[:, lo : lo + TQ],
            (((0,), (0,)), ((), ())),
            preferred_element_type=jnp.float32,
        )
        sides = []
        for n in range(2):
            part = scores[n * W : n * W + 3 * W, n * W : n * W + W]
            part = part * (SCALE * math.log2(math.e)) + bias_ref[2 * t + n]
            shifted = jnp.exp2(part - jnp.max(part, axis=0, keepdims=True))
            probs = shifted * (1.0 / jnp.sum(shifted, axis=0, keepdims=True))
            probs = probs.astype(jnp.bfloat16)
            sides.append(jnp.concatenate([blank, probs] if n else [probs, blank], axis=0))
        probs = jnp.concatenate(sides, axis=1)
        pieces.append(
            jnp.dot(v_t[:, lo : lo + TK], probs, preferred_element_type=jnp.float32).astype(
                jnp.bfloat16
            )
        )
    return jnp.concatenate(pieces, axis=1)


def pick(index, options):
    value = options[0]
    for k, option in enumerate(options[1:], 1):
        value = jnp.where(index == k, option, value)
    return value


N_COPIES = 128
LINE = (-1, 1, 2)
KEYS, REST = 0, 1
PART_ROWS = (HD, 2 * HD)


def body(len_ref, frames_hbm, gain_ref, wk_ref, wv_ref, wq_ref, wo_ref, out_hbm, frames, out, raw, pad, low, high, given, zk, zr, wk, wr, oline, obuf, wo, x_t, kbuf, bias, att, in_sem, out_sem, send_sem, recv_sem):
    dp = lax.axis_index("dp")
    tm = lax.axis_index("tm")
    x, y = dp // 2, (tm // 16) * 2 + dp % 2
    z, core = (tm // 2) % 8, tm % 2

    def device(px, py, pz, pc):
        return (px * 2 + py % 2, (py // 2) * 16 + pz * 2 + pc)

    def moved(first, second):
        dx = jnp.where(core == 0, first, second)
        dy = jnp.where(core == 0, second, first)
        return (x + dx + 4) % 4, (y + dy + 4) % 4

    def plane_device(first, second):
        px, py = moved(first, second)
        return device(px, py, z, core)

    def plane_place(first, second):
        px, py = moved(first, second)
        return px * 4 + py

    partner = device(x, y, 1 * z, 1 - core)
    z_line = {k: device(x, y, (z + k + 8) % 8, core) for k in (4, 3, -3, 2, -2, 1, -1)}
    after, before = (dp, (tm + 1) % 32), (dp, (tm + 31) % 32)
    first_line = {k: plane_device(k, 0) for k in LINE}
    second_line = {k: plane_device(0, k) for k in LINE}
    peers = [*first_line.values(), *second_line.values(), *z_line.values(), partner, after, before]

    fetch = pltpu.make_async_copy(frames_hbm, frames, in_sem)
    fetch.start()
    barrier = pltpu.get_barrier_semaphore()
    for peer in peers:
        pl.semaphore_signal(barrier, inc=1, device_id=peer, device_id_type=MESH)

    raw[...] = jnp.zeros_like(raw)
    for n, ref in enumerate((wk_ref, wv_ref, wq_ref, wo_ref)):
        raw[8 * n : 8 * n + 6] = ref[...].astype(jnp.float32)
    pad[0] = raw[:, :HALF].astype(jnp.bfloat16)
    pad[1] = raw[:, HALF:].astype(jnp.bfloat16)
    pl.semaphore_wait(barrier, len(peers))

    copies = {}

    def send(name, src, dst, peer):
        k = len(copies)
        copies[name] = pltpu.make_async_remote_copy(
            src_ref=src,
            dst_ref=dst,
            send_sem=send_sem.at[k],
            recv_sem=recv_sem.at[k],
            device_id=peer,
            device_id_type=MESH,
        )
        copies[name].start()

    def arrived(*names):
        for name in names:
            copies[name].wait_recv()

    send("swap", pad.at[1 - core], given, partner)

    first_pos = tm * ROWS
    length = len_ref[0]
    gain = gain_ref[...].reshape(1, D)

    def norm_block(ref, r, col):
        x_t[:, col : col + W] = norm_rows(ref[r : r + W], gain).T

    arrived("swap")
    mine, other = pad[core], given[...]
    one = jnp.where(core == 0, mine, other)
    two = jnp.where(core == 0, other, mine)
    own = plane_place(0, 0)
    zk[z] = jnp.concatenate([one[:8], two[:8]], axis=0)
    for k, peer in z_line.items():
        send(f"zk{k}", zk.at[z], zk.at[z], peer)
    along = jnp.where(core == 0, x, y)
    across = jnp.where(core == 0, y, x)
    oline[along] = jnp.concatenate([one[24:], two[24:]], axis=0)
    for k in LINE:
        send(f"of{k}", oline.at[along], oline.at[along], first_line[k])
    row = lax.broadcasted_iota(jnp.int32, (24, 32), 0)
    col = lax.broadcasted_iota(jnp.int32, (24, 32), 1)
    order = jnp.where(col == (row // 6) * 8 + row % 6, 1.0, 0.0).astype(jnp.bfloat16)
    packed = jnp.dot(
        order,
        jnp.concatenate([one[8:24], two[8:24]], axis=0),
        preferred_element_type=jnp.float32,
    )
    zr[z, :, :HALF] = packed[:16].astype(jnp.bfloat16)
    zr[z, :, HALF:] = jnp.concatenate(
        [packed[16:, : HALF // 2], packed[16:, HALF // 2 :]], axis=0
    ).astype(jnp.bfloat16)
    fetch.wait()

    norm_block(frames, 0, W)
    norm_block(frames, W, 2 * W)

    def chosen(rows, source, buf):
        col = lax.broadcasted_iota(jnp.int32, (rows, buf.shape[0]), 1)
        order = jnp.where(col == source, 1.0, 0.0).astype(jnp.bfloat16)
        return jnp.dot(order, buf, preferred_element_type=jnp.float32)

    def ordered_keys():
        row = lax.broadcasted_iota(jnp.int32, (HD, 8 * 16), 0)
        source = (row // 12) * 16 + (row % 12 // 6) * 8 + row % 6
        return chosen(HD, source, zk[...].reshape(8 * 16, HALF)).astype(jnp.bfloat16)

    def ordered_rest():
        row = lax.broadcasted_iota(jnp.int32, (2 * HD, 8 * 16), 0)
        kind, chip, part = row // HD, (row % HD) // 12, row % 12
        local = (part // 6) * 12 + kind * 6 + part % 6
        base = chip * 16
        wide = zr[:, :, :HALF].reshape(8 * 16, HALF)
        tail = zr[:, :, HALF:].reshape(8 * 16, HALF // 2)
        first = chosen(2 * HD, jnp.where(local < 16, base + local, -1), wide)
        left = chosen(2 * HD, jnp.where(local < 16, -1, base + local - 16), tail)
        right = chosen(2 * HD, jnp.where(local < 16, -1, base + local - 8), tail)
        return (first + jnp.concatenate([left, right], axis=1)).astype(jnp.bfloat16)

    parts = (wk, wr)

    def slab(name, part, first, second, peer, lo=0, size=None):
        ref = parts[part].at[plane_place(first, second), core]
        if size is not None:
            ref = parts[part].at[plane_place(first, second), core, pl.ds(lo, size)]
        send(f"{name},{part}", ref, ref, peer)

    def share(part, first, second):
        slab(f"c{first},{second}", part, first, second, partner)

    def begin(part):
        slab("f-", part, 0, 0, first_line[1])
        slab("f+", part, 0, 0, first_line[-1])
        slab("s0-", part, 0, 0, second_line[1])
        slab("s0+", part, 0, 0, second_line[-1])
        share(part, 0, 0)

    def first_step(part):
        half = PART_ROWS[part] // 2
        arrived(f"f-,{part}", f"f+,{part}")
        slab("ff-", part, -1, 0, first_line[1], 0, half)
        slab("ff+", part, 1, 0, first_line[-1], half, half)
        share(part, -1, 0)
        share(part, 1, 0)

    def second_begin(part, i):
        slab(f"s{i}-", part, i, 0, second_line[1])
        slab(f"s{i}+", part, i, 0, second_line[-1])

    def first_end(part):
        arrived(f"ff-,{part}", f"ff+,{part}")
        share(part, 2, 0)

    def second_step(part, i):
        half = PART_ROWS[part] // 2
        arrived(f"s{i}-,{part}", f"s{i}+,{part}")
        slab(f"ss{i}-", part, i, -1, second_line[1], 0, half)
        slab(f"ss{i}+", part, i, 1, second_line[-1], half, half)
        share(part, i, -1)
        share(part, i, 1)

    def second_end(part, i):
        arrived(f"ss{i}-,{part}", f"ss{i}+,{part}")
        share(part, i, 2)

    def locate(k, offsets, n, together):
        first = pick(k, [o[0] for o in offsets[n::together]])
        second = pick(k, [o[1] for o in offsets[n::together]])
        px, py = moved(first, second)
        return px * 4 + py, px * 4 + (py % 2) * 2 + py // 2

    def project(ref, places):
        rows = jnp.concatenate(
            [jnp.concatenate([ref[place, 0], ref[place, 1]], axis=1) for place in places], axis=0
        )
        return jnp.dot(rows, x_t[...], preferred_element_type=jnp.float32).astype(jnp.bfloat16)

    def keys(*offsets):
        arrived(*(f"c{second},{first},{KEYS}" for first, second in offsets))

        def some_keys(k, carry):
            places, names = zip(*(locate(k, offsets, n, 2) for n in range(2)))
            k_t = project(wk, places)
            for n in range(2):
                kbuf[names[n]] = k_t[n * HD : (n + 1) * HD]
            return carry

        lax.fori_loop(0, len(offsets) // 2, some_keys, 0)

    def heads(*offsets):
        arrived(*(f"c{second},{first},{REST}" for first, second in offsets))
        together = 2 - len(offsets) % 2

        def some_heads(k, carry):
            places, names = zip(*(locate(k, offsets, n, together) for n in range(together)))
            vq = project(wr, places)
            for n in range(together):
                v_t, q_t = (vq[(2 * n + m) * HD : (2 * n + m + 1) * HD] for m in range(2))
                att[names[n]] = attend_head(q_t[:, W : W + ROWS], kbuf[names[n]], v_t, bias)
            return carry

        lax.fori_loop(0, len(offsets) // together, some_heads, 0)

    def o_send(name, place, half, peer):
        ref = obuf.at[core, place, pl.ds(2 * half, 2)]
        send(f"{name}{half}", ref, ref, peer)

    def o_share(k):
        ref = obuf.at[core, (z + k + 8) % 8]
        send(f"oc{k}", ref, ref, partner)

    def o_begin():
        arrived(*(f"os{k}" for k in LINE))
        for half in range(2):
            o_send("ou1.", z, half, z_line[1])
            o_send("od1.", z, half, z_line[-1])
        o_share(0)

    def o_ring(d, half):
        arrived(f"ou{d}.{half}", f"od{d}.{half}")
        below, above = (z + 8 - d) % 8, (z + d) % 8
        if d < 3 or half == 0:
            o_send(f"ou{d + 1}.", below, half, z_line[1])
        if d < 3 or half == 1:
            o_send(f"od{d + 1}.", above, half, z_line[-1])
        if half == 1:
            o_share(-d)
            o_share(d)

    def o_end():
        arrived("ou4.0", "od4.1")
        o_share(4)

    arrived(*(f"zk{k}" for k in z_line))
    for k, peer in z_line.items():
        send(f"zr{k}", zr.at[z], zr.at[z], peer)
    wk[own, core] = ordered_keys()
    begin(KEYS)
    arrived(*(f"of{k}" for k in LINE))
    row = lax.broadcasted_iota(jnp.int32, (48, 64), 0)
    col = lax.broadcasted_iota(jnp.int32, (48, 64), 1)
    order = jnp.where(col == (row // 6) * 8 + row % 6, 1.0, 0.0).astype(jnp.bfloat16)
    obuf[core, z, across] = jnp.dot(
        order, oline[...].reshape(64, HALF), preferred_element_type=jnp.float32
    ).astype(jnp.bfloat16)
    for k in LINE:
        send(f"os{k}", obuf.at[core, z, across], obuf.at[core, z, across], second_line[k])
    norm_block(frames, 2 * W, 3 * W)
    first_step(KEYS)
    second_step(KEYS, 0)
    second_begin(KEYS, -1)
    second_begin(KEYS, 1)
    norm_block(frames, 3 * W, 4 * W)
    for t in range(ROWS // W):
        key = lax.broadcasted_iota(jnp.int32, (3 * W, W), 0)
        query = lax.broadcasted_iota(jnp.int32, (3 * W, W), 1)
        key_pos = key + (first_pos + (t - 1) * W)
        allowed = (
            (key - query >= 0) & (key - query <= 2 * W) & (key_pos >= 0) & (key_pos < length)
        )
        bias[t] = jnp.where(allowed, 0.0, -1e9).astype(jnp.float32)
    arrived(*(f"zr{k}" for k in z_line))
    wr[own, core] = ordered_rest()
    begin(REST)
    send("low", frames_hbm.at[pl.ds(ROWS - W, W)], low, after)
    send("high", frames_hbm.at[pl.ds(0, W)], high, before)
    o_begin()
    first_end(KEYS)
    second_begin(KEYS, 2)
    second_end(KEYS, 0)
    second_step(KEYS, -1)
    second_step(KEYS, 1)
    arrived("low", "high")
    norm_block(low, 0, 0)
    norm_block(high, 0, W + ROWS)
    second_step(KEYS, 2)
    second_end(KEYS, -1)
    second_end(KEYS, 1)
    keys((0, 0), (-1, 0), (1, 0), (0, -1), (0, 1), (2, 0))
    first_step(REST)
    second_step(REST, 0)
    second_begin(REST, -1)
    second_begin(REST, 1)
    o_ring(1, 0)
    heads((0, 0))
    second_end(KEYS, 2)
    o_ring(1, 1)
    keys((0, 2), (-1, -1), (1, 1), (-1, 1))
    first_end(REST)
    second_begin(REST, 2)
    second_end(REST, 0)
    o_ring(2, 0)
    heads((-1, 0), (1, 0))
    o_ring(2, 1)
    second_step(REST, -1)
    heads((0, -1), (0, 1))
    second_step(REST, 1)
    o_ring(3, 0)
    heads((2, 0), (0, 2))
    o_ring(3, 1)
    second_end(REST, -1)
    keys((1, -1), (2, -1), (2, 1), (-1, 2), (1, 2), (2, 2))
    second_step(REST, 2)
    heads((-1, -1), (1, 1))
    second_end(REST, 1)
    o_end()
    heads((-1, 1), (1, -1))
    heads((2, -1), (-1, 2))
    second_end(REST, 2)
    heads((2, 1), (1, 2))
    arrived(*(f"oc{k}" for k in range(-3, 5)))
    row = lax.broadcasted_iota(jnp.int32, (4 * HD, 8 * 48), 0)
    col = lax.broadcasted_iota(jnp.int32, (4 * HD, 8 * 48), 1)
    unit, part = (row % HD) // 12, row % 12
    order = jnp.where(col == unit * 48 + (row // HD) * 12 + part, 1.0, 0.0).astype(jnp.bfloat16)
    for half in range(2):
        for fixed in range(4):
            four = jnp.dot(
                order,
                obuf[half, :, fixed].reshape(8 * 48, HALF),
                preferred_element_type=jnp.float32,
            ).astype(jnp.bfloat16)
            for k in range(4):
                px, py = (fixed, k) if half else (k, fixed)
                head = px * 4 + (py % 2) * 2 + py // 2
                wo[head, :, half * HALF : (half + 1) * HALF] = four[k * HD : (k + 1) * HD]
    heads((2, 2))

    att_rows = att[...].reshape(D, ROWS).T
    pos = first_pos + lax.broadcasted_iota(jnp.int32, (ROWS, 1), 0)
    stores = []
    for n, c in enumerate(range(0, H, 4)):
        mixed = lax.dot_general(
            att_rows,
            wo[c : c + 4].reshape(4 * HD, D),
            (((1,), (1,)), ((), ())),
            preferred_element_type=jnp.float32,
        )
        cols = pl.ds(c * HD, 4 * HD)
        summed = frames[:, cols].astype(jnp.float32) + mixed
        out[:, cols] = jnp.where(pos < length, summed, 0.0).astype(jnp.bfloat16)
        stores.append(pltpu.make_async_copy(out.at[:, cols], out_hbm.at[:, cols], out_sem.at[n]))
        stores[-1].start()

    for copy in copies.values():
        copy.wait_send()
    for store in stores:
        store.wait()


def per_device(frames, lengths, ln_gain, w_query, w_key, w_value, w_out):
    vmem = pl.BlockSpec(memory_space=pltpu.VMEM)
    anywhere = pl.BlockSpec(memory_space=pl.ANY)
    bf16 = jnp.bfloat16
    result = pl.pallas_call(
        body,
        out_shape=jax.ShapeDtypeStruct((ROWS, D), bf16),
        in_specs=[pl.BlockSpec(memory_space=pltpu.SMEM), anywhere, vmem, vmem, vmem, vmem, vmem],
        out_specs=anywhere,
        scratch_shapes=[
            pltpu.VMEM((ROWS, D), bf16),
            pltpu.VMEM((ROWS, D), bf16),
            pltpu.VMEM((32, D), jnp.float32),
            pltpu.VMEM((2, 32, HALF), bf16),
            pltpu.VMEM((W, D), bf16),
            pltpu.VMEM((W, D), bf16),
            pltpu.VMEM((32, HALF), bf16),
            pltpu.VMEM((8, 16, HALF), bf16),
            pltpu.VMEM((8, 16, 3 * HALF // 2), bf16),
            pltpu.VMEM((H, 2, HD, HALF), bf16),
            pltpu.VMEM((H, 2, 2 * HD, HALF), bf16),
            pltpu.VMEM((4, 16, HALF), bf16),
            pltpu.VMEM((2, 8, 4, 48, HALF), bf16),
            pltpu.VMEM((H, HD, D), bf16),
            pltpu.VMEM((D, EXT), bf16),
            pltpu.VMEM((H, HD, EXT), bf16),
            pltpu.VMEM((ROWS // W, 3 * W, W), jnp.float32),
            pltpu.VMEM((H, HD, ROWS), bf16),
            pltpu.SemaphoreType.DMA,
            pltpu.SemaphoreType.DMA((4,)),
            pltpu.SemaphoreType.DMA((N_COPIES,)),
            pltpu.SemaphoreType.DMA((N_COPIES,)),
        ],
        compiler_params=pltpu.CompilerParams(
            collective_id=0, has_side_effects=True, vmem_limit_bytes=60 * 2**20
        ),
    )(lengths, frames[0], ln_gain, w_key.T, w_value.T, w_query.T, w_out.T)
    return result[None]


def solution(mesh):
    in_specs = (
        P("dp", "tm", None),
        P("dp"),
        P(),
        P(None, ("dp", "tm")),
        P(None, ("dp", "tm")),
        P(None, ("dp", "tm")),
        P(None, ("dp", "tm")),
    )
    return jax.shard_map(
        per_device,
        mesh=mesh,
        in_specs=in_specs,
        out_specs=P("dp", "tm", None),
        check_vma=False,
    )
```
